256 devices in a mesh: img: 128 (over y, x, z), chan: 2 (over core).
Axes of the slice: x: 4, y: 4, z: 8, core: 2. Of those that a mesh axis runs over, the one named last changes fastest.
Arguments:
- visibilities: bfloat16 [2, 2, 2097152], P('chan', None, 'img'), may hold values from -6 to 6
- owner: int32 [2, 2097152, 1], P('chan', 'img'), may hold values from 0 to 127; in each aligned block of 16384 rows (0 to 16383, 16384 to 32767, ..., all dimensions but the last counted through in order) at most 256 rows name the same one
- cells: int32 [2, 2, 2097152], P('chan', None, 'img'), may hold values from 0 to 248
- taps: int32 [2, 2, 2097152], P('chan', None, 'img'), may hold values from 0 to 127
- kernel: bfloat16 [128, 8], replicated, may hold values from 0.099609375 to 1
- taper_rows: float32 [32768], P('img'), may hold values from 0.1 to 1.9
- taper_cols: float32 [256], P('chan'), may hold values from 0.1 to 1.9
Outputs:
- image: float32 [2, 32768, 256], P(None, 'img', 'chan')
The draws below stay inside these ranges and needn't reach their ends.
Inputs may be any that keep to these rules, and one draw needn't show every extreme that they name: `owner`: among the visibilities of one channel held by one device, no subgrid is named more than 256 times, and in some device's rows one subgrid is named exactly 256 times.
All inputs are finite; a program needn't handle non-finite values.
Results may differ from the reference program's by a relative error of at most 0.0029.
Values may be sent and summed in bfloat16 or wider, within the bound.
A program may use at most 128 MiB of HBM per device.

```python
import math
import jax
import jax.numpy as jnp
import numpy as np
from jax import lax

SUB = 256
TAPS = 8
OS = 128
VIS_DEV = 16384
CAP = 256
CHANNELS = 2
ROWS = 2097152
NU = 32768
N_IMG = 128


def set_ends(entries, key, low, largest):
    longest = entries.shape.index(max(entries.shape))
    spots = []
    for shift in (0, 1):
        where = [jax.random.randint(jax.random.fold_in(key, axis), (), 0, length) for axis, length in enumerate(entries.shape)]
        where[longest] = (where[longest] + shift) % entries.shape[longest]
        spots.append(tuple(where))
    return entries.at[spots[0]].set(low).at[spots[1]].set(largest)


def shard_levels(key, dims, pieces, low, high):
    loudness, own = 1.0, jax.random.fold_in(key, 6)
    for dim, parts in pieces:
        steps = jnp.exp(jax.random.uniform(jax.random.fold_in(own, dim), (parts,), jnp.float32, low / len(pieces), high / len(pieces)))
        loudness = loudness * jnp.repeat(steps, dims[dim] // parts).reshape([-1 if axis == dim else 1 for axis in range(len(dims))])
    return loudness


def assign_block(own_key, own, number, rows, count, top, most, slope):
    ranking = jax.random.permutation(own_key, count)
    crowded, ordinary = load_shares(count, rows * top, most, slope, True), load_shares(count, rows * top, most, slope, False)
    places = jnp.arange(count)

    def named(sizes, rotation):
        used = int((sizes > 0).sum())
        fixed = max(1, used // 4)
        shifted = fixed + (places - fixed + rotation * (used - fixed)) % max(1, count - fixed)
        return jnp.zeros((count,), jnp.int32).at[ranking[jnp.where(places < fixed, places, shifted)]].set(jnp.asarray(sizes, jnp.int32))

    sizes = jnp.where(number % 4 == 0, named(crowded, number // 4), named(ordinary, number - number // 4 - 1))
    mixed = jax.random.permutation(jax.random.fold_in(own, 3), count)
    source_of, sink = mixed[0:count // 2 * 2:2], mixed[1:count // 2 * 2:2]
    slack = jnp.minimum(sizes[source_of] - 1, most - sizes[sink]) // 2
    slack = jnp.where((source_of == ranking[0]) | (sink == ranking[0]) | (sizes[sink] == 0), 0, jnp.maximum(slack, 0))
    shifted = jax.random.randint(jax.random.fold_in(own, 4), (count // 2,), 0, 1 << 20) % (slack + 1)
    sizes = sizes.at[source_of].add(-shifted).at[sink].add(shifted)
    members = jnp.searchsorted(jnp.cumsum(sizes), jnp.arange(rows * top), side="right").astype(jnp.int32)
    table = members.reshape(top, rows).T
    table = table[jax.random.permutation(jax.random.fold_in(own, 1), rows)]
    rotation = jax.random.randint(jax.random.fold_in(own, 2), (rows, 1), 0, top)
    return jnp.take_along_axis(table, (jnp.arange(top)[None, :] + rotation) % top, axis=1)


def load_shares(count, total, reach, slope, full):
    portions = [(1 << 20) // math.isqrt(grade ** slope) + 1 for grade in range(1, count + 1)]
    largest = reach if full else min(reach, max(-(-total // count), total * portions[0] // sum(portions)))
    least = 1 if total - largest >= count - 1 else 0
    given, rest = [largest] + [least] * (count - 1), total - largest - least * (count - 1)
    while rest > 0:
        free = [i for i in range(1, count) if given[i] < largest] or [i for i in range(1, count) if given[i] < reach]
        whole, budget = sum([portions[i] for i in free]), rest
        for i in free:
            extra = min(reach - given[i], max(1, budget * portions[i] // whole), rest)
            given[i] = given[i] + extra
            rest = rest - extra
    return np.array(given)


def bell_draw(stream_key, dims, scale, most, split=(), kind=jnp.bfloat16):
    result = jax.random.normal(stream_key, dims, jnp.float32) * scale
    if len(split) > 0:
        result = shard_levels(stream_key, dims, split, -0.22, 0.18) * result
    return jnp.clip(result, min=-most, max=most).astype(kind)


def setup_inputs(seed: int = 0) -> dict:
    key_list = jax.random.split(jax.random.key(seed), 8)
    visibilities = bell_draw(key_list[0], (CHANNELS, 2, ROWS), 1.0, 6.0, ((0, 2), (2, 128)))
    owner_keys = jax.random.split(jax.random.fold_in(key_list[1], 1), CHANNELS * ROWS // VIS_DEV)
    owner_turns = jax.random.permutation(jax.random.fold_in(key_list[1], 3), CHANNELS * ROWS // VIS_DEV)
    owner = jax.vmap(lambda own, number: assign_block(jax.random.fold_in(key_list[1], 2), own, number, VIS_DEV, N_IMG, 1, CAP, 2))(owner_keys, owner_turns).reshape((CHANNELS, ROWS, 1))
    cells = set_ends(jax.random.randint(key_list[2], (CHANNELS, 2, ROWS), 0, SUB - TAPS + 1), jax.random.fold_in(key_list[2], 1), 0, SUB - TAPS).astype(jnp.int32)
    taps = set_ends(jax.random.randint(key_list[3], (CHANNELS, 2, ROWS), 0, OS), jax.random.fold_in(key_list[3], 1), 0, OS - 1).astype(jnp.int32)
    kernel = jnp.clip(jax.random.uniform(key_list[4], (OS, TAPS), jnp.float32, 0.099609375, 1.0), 0.099609375, 1.0).astype(jnp.bfloat16)
    taper_rows = jnp.clip(1.0 + 0.18 * jax.random.normal(key_list[5], (NU,), jnp.float32), 0.1, 1.9)
    taper_cols = jnp.clip(1.0 + 0.18 * jax.random.normal(key_list[6], (SUB,), jnp.float32), 0.1, 1.9)
    return dict(visibilities=visibilities, owner=owner, cells=cells, taps=taps, kernel=kernel, taper_rows=taper_rows, taper_cols=taper_cols)


def rounded(value):
    narrow = lax.optimization_barrier(value.astype(jnp.bfloat16))
    return narrow.astype(jnp.float32)

def channel_grid(inputs, kernel_table):
    vis_pair, owners, cell_pair, tap_pair = inputs
    ku_rows = kernel_table[tap_pair[0]]
    kv_rows = kernel_table[tap_pair[1]]
    vis_float = vis_pair.astype(jnp.float32)
    weight_re = rounded(vis_float[0][:, None] * ku_rows)
    weight_im = rounded(vis_float[1][:, None] * ku_rows)
    tap_range = jnp.arange(TAPS, dtype=jnp.int32)
    u_start = owners[:, 0].astype(jnp.int32) * SUB + cell_pair[0].astype(jnp.int32)
    u_index = u_start[:, None, None] + tap_range[None, :, None]
    v_index = cell_pair[1].astype(jnp.int32)[:, None, None] + tap_range[None, None, :]
    patch_re = weight_re[:, :, None] * kv_rows[:, None, :]
    patch_im = weight_im[:, :, None] * kv_rows[:, None, :]
    u_full = jnp.broadcast_to(u_index, patch_re.shape)
    v_full = jnp.broadcast_to(v_index, patch_re.shape)
    grid_re = jnp.zeros((NU, SUB), jnp.float32).at[u_full, v_full].add(patch_re)
    grid_im = jnp.zeros((NU, SUB), jnp.float32).at[u_full, v_full].add(patch_im)
    return (grid_re, grid_im)

def reference(visibilities, owner, cells, taps, kernel, taper_rows, taper_cols):
    kernel_table = kernel.astype(jnp.float32)
    grids_re, grids_im = lax.map(lambda inputs: channel_grid(inputs, kernel_table), (visibilities, owner, cells, taps))
    field = lax.optimization_barrier(jnp.sum(grids_re, axis=0)) + 1j * lax.optimization_barrier(jnp.sum(grids_im, axis=0))
    spectrum = jnp.fft.ifft2(field) * math.sqrt(NU * SUB)
    bit_count = N_IMG.bit_length() - 1
    positions = np.arange(N_IMG)
    order = np.zeros(N_IMG, np.int32)
    for bit_index in range(bit_count):
        order = order | ((positions >> bit_index & 1) << bit_count - 1 - bit_index).astype(np.int32)
    arranged = spectrum.reshape(SUB, N_IMG, SUB).transpose(1, 0, 2)[order].reshape(NU, SUB)
    factor = taper_rows[:, None] * taper_cols[None, :]
    image = jnp.stack([jnp.real(arranged) * factor, jnp.imag(arranged) * factor])
    return image.astype(jnp.float32)
```

```python
import functools
import math

import jax
import jax.numpy as jnp
import numpy as np
from jax import lax
from jax.experimental import pallas as pl
from jax.experimental.pallas import tpu as pltpu
from jax.sharding import PartitionSpec as P

SUB = 256
TAPS = 8
OS = 128
IMG = 128
HALF = 128
CAP = 256
VIS = 16384
CHUNK = 2048
GROUP = 16
F32 = jnp.float32
BF16 = jnp.bfloat16
MESH = pl.DeviceIdType.MESH


def split_table(table):
    high = table.astype(np.float32).astype(jnp.bfloat16)
    low = (table - high.astype(np.float64)).astype(np.float32).astype(jnp.bfloat16)
    return np.stack([high, low])


def reversed_bits(count):
    bits = count.bit_length() - 1
    positions = np.arange(count)
    order = np.zeros(count, np.int64)
    for bit in range(bits):
        order |= (positions >> bit & 1) << bits - 1 - bit
    return order


@functools.lru_cache(maxsize=None)
def host_tables():
    points = np.arange(SUB)
    angle = 2 * np.pi * (points[:, None] * points[None, :] % SUB) / SUB
    cosine, sine = np.cos(angle), np.sin(angle)
    halves = [
        np.concatenate([cosine[:, h * HALF : (h + 1) * HALF], sine[:, h * HALF : (h + 1) * HALF]], 1)
        for h in (0, 1)
    ]
    v_tables = split_table(np.stack(halves))
    order = reversed_bits(IMG)
    places = np.arange(IMG)
    turn = 2 * np.pi * (order[:, None] * places[None, :] % IMG) / IMG
    across = np.stack([np.stack([np.cos(turn), -np.sin(turn)], -1), np.stack([np.sin(turn), np.cos(turn)], -1)], 1)
    u_table = np.einsum("apoq,hg->aphoqg", across, np.eye(2)).reshape(4 * IMG, 4 * IMG)
    u_tables = split_table(u_table)
    row = places[:, None, None] + np.zeros((1, 2, 1), np.int64) + IMG * np.arange(2)[None, None, :]
    quarter = np.zeros((IMG, 1, 1)) + np.arange(2)[None, :, None] + np.zeros((1, 1, 2))
    row, quarter = row.reshape(-1), quarter.reshape(-1)
    last = 2 * np.pi * (points[:, None] * row[None, :] % SUB) / SUB + quarter[None, :] * np.pi / 2
    last_tables = np.stack([np.cos(last), np.sin(last)]).astype(np.float32)
    twist = 2 * np.pi * (order[:, None] * row[None, :]) / (IMG * SUB)
    twists = np.stack([np.cos(twist), np.sin(twist)], 1).astype(np.float32)
    return v_tables, u_tables, last_tables, twists


def dot_nt(left, right):
    return lax.dot_general(left, right, (((1,), (1,)), ((), ())), preferred_element_type=F32)


def dot_nn(left, right):
    return lax.dot_general(left, right, (((1,), (0,)), ((), ())), preferred_element_type=F32)


def split_pair(value):
    high = value.astype(BF16)
    low = (value - high.astype(F32)).astype(BF16)
    return high, low


def bucket(vis_ref, own_ref, cells_ref, taps_ref, out_ref, acc, lhs, rhs):
    acc[...] = jnp.zeros_like(acc)
    first = lax.broadcasted_iota(jnp.int32, (SUB, SUB), 0)
    second = lax.broadcasted_iota(jnp.int32, (SUB, SUB), 1)
    upper = jnp.where(first <= second, 1.0, 0.0).astype(BF16)
    names = lax.broadcasted_iota(jnp.int32, (IMG, CHUNK), 0)
    lines = lax.broadcasted_iota(jnp.int32, (16, CHUNK), 0)
    lower_half = jnp.where(lines >= 8, 1.0, 0.0)
    lines = lines.astype(F32)
    zero = jnp.zeros((16, CHUNK), BF16)
    one = jnp.ones((16, CHUNK), BF16)

    def step(turn, carry):
        columns = pl.ds(pl.multiple_of(turn * CHUNK, CHUNK), CHUNK)
        owners = own_ref[:, columns]
        named = jnp.where(names == owners, 1.0, 0.0)
        marks = named.astype(BF16)
        ranks = []
        for part in range(CHUNK // SUB):
            span = slice(part * SUB, (part + 1) * SUB)
            counts = dot_nn(marks[:, span], upper) + carry
            ranks.append(jnp.sum(named[:, span] * counts, axis=0, keepdims=True) - 1.0)
            carry = counts[:, SUB - 1 : SUB]
        rank = jnp.concatenate(ranks, axis=1)
        gap = (rank - lines).astype(BF16)
        for block in range(CAP // 16):
            rhs[block * 16 : (block + 1) * 16, :] = jnp.where(gap == block * 16, one, zero)
        features = jnp.concatenate(
            [
                vis_ref[:, columns].astype(F32),
                cells_ref[:, columns].astype(F32),
                taps_ref[:, columns].astype(F32),
                jnp.zeros((2, CHUNK), F32),
            ],
            axis=0,
        )
        features = jnp.concatenate([features, features], axis=0).astype(BF16)
        owner_gap = (owners.astype(F32) - lower_half).astype(BF16)
        for block in range(IMG // 2):
            lhs[block * 16 : (block + 1) * 16, :] = jnp.where(owner_gap == 2 * block, features, zero)
        acc[...] += dot_nt(lhs[...], rhs[...])
        return carry

    lax.fori_loop(0, VIS // CHUNK, step, jnp.zeros((IMG, 1), F32))
    total = acc[...]
    front = total[:, :HALF].reshape(IMG, 8, HALF)
    back = total[:, HALF:].reshape(IMG, 8, HALF)
    out_ref[...] = jnp.concatenate([front, back], axis=1).astype(BF16)


def spread(table, cell, tap, lines):
    block = jnp.floor(cell * 0.125)
    low = cell - block * 8.0
    gap = lines - low
    wraps = gap < 0.0
    source = jnp.where(wraps, gap + 8.0, gap).astype(jnp.int32)
    looked = jnp.take_along_axis(table, tap.astype(jnp.int32), axis=1)
    turned = jnp.take_along_axis(looked, source, axis=0)
    return turned, block + jnp.where(wraps, 1.0, 0.0)


def grid_group(arrived, start, table, lhs, rhs):
    lines = lax.broadcasted_iota(jnp.int32, (8, HALF), 0).astype(F32)
    zero = jnp.zeros((16, HALF), BF16)
    for source in range(GROUP):
        message = arrived[start + source].astype(F32)
        for half in range(2):
            slots = message[half * 8 : half * 8 + 8]
            columns = slice((source * 2 + half) * HALF, (source * 2 + half + 1) * HALF)

            def line(index):
                return jnp.broadcast_to(slots[index : index + 1], (8, HALF))

            turned_u, block_u = spread(table, line(2), line(4), lines)
            turned_v, block_v = spread(table, line(3), line(5), lines)
            real, imag = line(0) * turned_u, line(1) * turned_u
            real = jnp.concatenate([real, real], axis=0).astype(BF16)
            imag = jnp.concatenate([imag, imag], axis=0).astype(BF16)
            weight_v = jnp.concatenate([turned_v, turned_v], axis=0).astype(BF16)
            at_u = jnp.concatenate([block_u, block_u - 1.0], axis=0).astype(BF16)
            at_v = jnp.concatenate([block_v, block_v - 1.0], axis=0).astype(BF16)
            for block in range(SUB // 16):
                here = at_u == 2 * block
                lhs[block * 16 : (block + 1) * 16, columns] = jnp.where(here, real, zero)
                lhs[SUB + block * 16 : SUB + (block + 1) * 16, columns] = jnp.where(here, imag, zero)
                rhs[block * 16 : (block + 1) * 16, columns] = jnp.where(at_v == 2 * block, weight_v, zero)


def main_kernel(
    vis_ref, own_ref, cells_ref, taps_ref, table_ref, rows_ref, cols_ref, v_ref, u_ref, last_ref, twist_ref, out_ref,
    big, lhs, rhs, lhs_grid, rhs_grid, sent, arrived, grid, cross_out, cross_in, out_two, in_two, out_three, in_three,
    final_table, factor, send_sem, recv_sem, cross_sem, far_send, far_recv, own_sem,
):
    me, chan = lax.axis_index("img"), lax.axis_index("chan")
    barrier = pltpu.get_barrier_semaphore()

    def greet(step, count):
        pl.semaphore_signal(barrier, inc=1, device_id=(lax.rem(me + step, IMG), chan), device_id_type=MESH)
        return count

    lax.fori_loop(1, IMG, greet, 0)
    pl.semaphore_signal(barrier, inc=1, device_id=(me, 1 - chan), device_id_type=MESH)

    bucket(vis_ref, own_ref, cells_ref, taps_ref, sent, big, lhs, rhs)

    pl.semaphore_wait(barrier, IMG)

    pltpu.make_async_copy(sent.at[me], arrived.at[0], own_sem.at[0]).start()

    def send_vis(step, count):
        peer = lax.rem(me + step, IMG)
        pltpu.make_async_remote_copy(
            src_ref=sent.at[peer], dst_ref=arrived.at[step], send_sem=send_sem,
            recv_sem=recv_sem.at[step // GROUP], device_id=(peer, chan), device_id_type=MESH,
        ).start()
        return count

    lax.fori_loop(1, IMG, send_vis, 0)

    cosine, sine = twist_ref[me, 0:1, :], twist_ref[me, 1:2, :]
    scale = 1.0 / math.sqrt(SUB * IMG * SUB)
    for block in range(2):
        rows = slice(block * HALF, (block + 1) * HALF)
        base_cos, base_sin = last_ref[0, rows, :], last_ref[1, rows, :]
        high, low = split_pair(base_cos * cosine - base_sin * sine)
        final_table[0, rows, :] = high
        final_table[1, rows, :] = low
        rows_low = slice(SUB + block * HALF, SUB + (block + 1) * HALF)
        high, low = split_pair(base_sin * cosine + base_cos * sine)
        final_table[0, rows_low, :] = high
        final_table[1, rows_low, :] = low
        column = jnp.transpose(jnp.broadcast_to(rows_ref[:, rows], (HALF, HALF)))
        factor[rows, :] = column * cols_ref[...] * scale

    grid[...] = jnp.zeros_like(grid)
    table = table_ref[...].astype(F32)

    def wait_span(count, semaphore):
        span = pl.ds(0, count)
        pltpu.make_async_remote_copy(
            src_ref=sent.at[span], dst_ref=arrived.at[span], send_sem=send_sem, recv_sem=semaphore,
            device_id=(me, 1 - chan), device_id_type=MESH,
        ).wait_recv()

    pltpu.make_async_copy(sent.at[me], arrived.at[0], own_sem.at[0]).wait()
    wait_span(GROUP - 1, recv_sem.at[0])

    def grid_step(group, count):
        @pl.when(group > 0)
        def _():
            wait_span(GROUP, recv_sem.at[group])

        grid_group(arrived, group * GROUP, table, lhs_grid, rhs_grid)
        grid[...] += dot_nt(lhs_grid[...], rhs_grid[...])
        return count

    lax.fori_loop(0, IMG // GROUP, grid_step, 0)

    grid_high, grid_low = split_pair(grid[...])

    def half_spectrum(half):
        high, low = v_ref[0, half], v_ref[1, half]
        both = dot_nn(grid_high, high) + (dot_nn(grid_high, low) + dot_nn(grid_low, high))
        real = both[:SUB, :HALF] - both[SUB:, HALF:]
        imag = both[:SUB, HALF:] + both[SUB:, :HALF]
        return jnp.concatenate([real, imag], axis=0)

    cross_out[...] = half_spectrum(1 - chan)
    cross = pltpu.make_async_remote_copy(
        src_ref=cross_out, dst_ref=cross_in, send_sem=cross_sem.at[0], recv_sem=cross_sem.at[1],
        device_id=(me, 1 - chan), device_id_type=MESH,
    )
    cross.start()
    mine = half_spectrum(chan)
    place = lax.broadcasted_iota(jnp.int32, (4 * IMG, 4 * IMG), 0)
    origin = lax.broadcasted_iota(jnp.int32, (4 * IMG, 4 * IMG), 1)
    swap = jnp.where(origin == (place & 3) * IMG + (place >> 2), 1.0, 0.0).astype(BF16)
    cross.wait_recv()
    summed = (mine + cross_in[...]).astype(BF16)
    out_two[...] = dot_nn(swap, summed).reshape(IMG, 4, HALF).astype(BF16)

    def exchange(source, target, phase):
        keep = pltpu.make_async_copy(source.at[me], target.at[me], own_sem.at[1 + phase])
        keep.start()

        def send(step, count):
            peer = lax.rem(me + step, IMG)
            pltpu.make_async_remote_copy(
                src_ref=source.at[peer], dst_ref=target.at[me], send_sem=far_send.at[phase],
                recv_sem=far_recv.at[phase], device_id=(peer, chan), device_id_type=MESH,
            ).start()
            return count

        lax.fori_loop(1, IMG, send, 0)
        keep.wait()
        span = pl.ds(0, IMG - 1)
        return pltpu.make_async_remote_copy(
            src_ref=source.at[span], dst_ref=target.at[span], send_sem=far_send.at[phase],
            recv_sem=far_recv.at[phase], device_id=(me, 1 - chan), device_id_type=MESH,
        )

    second = exchange(out_two, in_two, 0)
    second.wait_recv()
    columns = in_two[...].reshape(4 * IMG, HALF)
    lines = dot_nn(u_ref[0], columns) + dot_nn(u_ref[1], columns)
    out_three[...] = lines.reshape(IMG, 4, HALF).astype(BF16)
    third = exchange(out_three, in_three, 1)
    third.wait_recv()
    columns = in_three[...].reshape(4 * IMG, HALF)
    image = dot_nn(final_table[0], columns) + dot_nn(final_table[1], columns)
    out_ref[0] = image[:SUB] * factor[...]
    out_ref[1] = image[SUB:] * factor[...]

    span = pl.ds(0, IMG - 1)
    pltpu.make_async_remote_copy(
        src_ref=sent.at[span], dst_ref=arrived.at[span], send_sem=send_sem, recv_sem=recv_sem.at[0],
        device_id=(me, 1 - chan), device_id_type=MESH,
    ).wait_send()
    cross.wait_send()
    second.wait_send()
    third.wait_send()


def body(visibilities, owner, cells, taps, kernel, taper_rows, taper_cols):
    v_tables, u_tables, last_tables, twists = host_tables()
    return pl.pallas_call(
        main_kernel,
        out_shape=jax.ShapeDtypeStruct((2, SUB, HALF), F32),
        in_specs=[pl.BlockSpec(memory_space=pltpu.VMEM)] * 11,
        out_specs=pl.BlockSpec(memory_space=pltpu.VMEM),
        scratch_shapes=[
            pltpu.VMEM((8 * IMG, CAP), F32),
            pltpu.VMEM((8 * IMG, CHUNK), BF16),
            pltpu.VMEM((CAP, CHUNK), BF16),
            pltpu.VMEM((2 * SUB, GROUP * CAP), BF16),
            pltpu.VMEM((SUB, GROUP * CAP), BF16),
            pltpu.VMEM((IMG, 16, HALF), BF16),
            pltpu.VMEM((IMG, 16, HALF), BF16),
            pltpu.VMEM((2 * SUB, SUB), F32),
            pltpu.VMEM((2 * SUB, HALF), F32),
            pltpu.VMEM((2 * SUB, HALF), F32),
            pltpu.VMEM((IMG, 4, HALF), BF16),
            pltpu.VMEM((IMG, 4, HALF), BF16),
            pltpu.VMEM((IMG, 4, HALF), BF16),
            pltpu.VMEM((IMG, 4, HALF), BF16),
            pltpu.VMEM((2, 4 * IMG, 4 * IMG), BF16),
            pltpu.VMEM((SUB, HALF), F32),
            pltpu.SemaphoreType.DMA(()),
            pltpu.SemaphoreType.DMA((IMG // GROUP,)),
            pltpu.SemaphoreType.DMA((2,)),
            pltpu.SemaphoreType.DMA((2,)),
            pltpu.SemaphoreType.DMA((2,)),
            pltpu.SemaphoreType.DMA((3,)),
        ],
        compiler_params=pltpu.CompilerParams(
            collective_id=0, has_side_effects=True, vmem_limit_bytes=48 * 1024 * 1024
        ),
        name="gridding",
    )(
        visibilities[0], owner.reshape(1, VIS), cells[0], taps[0], kernel.T,
        taper_rows.reshape(1, SUB), taper_cols.reshape(1, HALF),
        jnp.asarray(v_tables), jnp.asarray(u_tables), jnp.asarray(last_tables), jnp.asarray(twists),
    )


def solution(mesh):
    return jax.shard_map(
        body,
        mesh=mesh,
        in_specs=(
            P("chan", None, "img"),
            P("chan", "img", None),
            P("chan", None, "img"),
            P("chan", None, "img"),
            P(),
            P("img"),
            P("chan"),
        ),
        out_specs=P(None, "img", "chan"),
        check_vma=False,
    )
```

```python
import functools
import math

import jax
import jax.numpy as jnp
import numpy as np
from jax import lax
from jax.experimental import pallas as pl
from jax.experimental.pallas import tpu as pltpu
from jax.sharding import PartitionSpec as P

SUB = 256
TAPS = 8
OS = 128
IMG = 128
HALF = 128
CAP = 256
VIS = 16384
CHUNK = 4096
BLOCK = 16
GROUP = 32
ORDER = (0, 7, 1, 6, 2, 5, 3, 4)
FAR = 72
F32 = jnp.float32
BF16 = jnp.bfloat16
MESH = pl.DeviceIdType.MESH


def split_table(table):
    high = table.astype(np.float32).astype(jnp.bfloat16)
    low = (table - high.astype(np.float64)).astype(np.float32).astype(jnp.bfloat16)
    return high, low


def reversed_bits(count):
    bits = count.bit_length() - 1
    positions = np.arange(count)
    order = np.zeros(count, np.int64)
    for bit in range(bits):
        order |= (positions >> bit & 1) << bits - 1 - bit
    return order


@functools.lru_cache(maxsize=None)
def host_tables():
    points = np.arange(SUB)
    angle = 2 * np.pi * (points[:, None] * points[None, :] % SUB) / SUB
    cosine, sine = np.cos(angle), np.sin(angle)
    halves = []
    for start in (0, HALF):
        half_cos, half_sin = cosine[:, start : start + HALF], sine[:, start : start + HALF]
        high, low = split_table(np.block([[half_cos, half_sin], [-half_sin, half_cos]]))
        halves.append(np.concatenate([high, low, high], axis=0))
    v_tables = np.stack(halves)
    order = reversed_bits(IMG)
    turn = 2 * np.pi * (order[:, None] * np.arange(IMG)[None, :] % IMG) / IMG
    each = np.eye(2)
    high, low = split_table(np.concatenate([np.kron(np.cos(turn), each), np.kron(np.sin(turn), each)], axis=0))
    u_table = np.concatenate([high, low], axis=1)
    last_tables = np.stack([cosine, sine]).astype(np.float32)
    twist = 2 * np.pi * (order[:, None] * points[None, :]) / (IMG * SUB)
    twists = np.stack([np.cos(twist), np.sin(twist)], 1).astype(np.float32)
    return v_tables, u_table, last_tables, twists


def dot_nt(left, right):
    return lax.dot_general(left, right, (((1,), (1,)), ((), ())), preferred_element_type=F32)


def dot_nn(left, right):
    return lax.dot_general(left, right, (((1,), (0,)), ((), ())), preferred_element_type=F32)


def split_pair(value):
    high = value.astype(BF16)
    low = (value - high.astype(F32)).astype(BF16)
    return high, low


def encode(cell, tap):
    code = jnp.full(cell.shape, 2.0**-124, F32)
    for bit in range(7):
        code = jnp.where((cell >> bit & 1) == 1, code * 2.0 ** (1 << bit), code)
    code = jnp.where(cell >> 7 == 1, code * 2.0**64 * 2.0**64, code)
    return code * (1.0 + tap.astype(F32) * (1.0 / OS))


def decode(code):
    cell = jnp.zeros(code.shape, F32)
    large = code >= 2.0**4
    code = jnp.where(large, code * 2.0**-64 * 2.0**-64, code)
    cell = jnp.where(large, cell + 128.0, cell)
    for bit in range(6, -1, -1):
        large = code >= 2.0 ** ((1 << bit) - 124)
        code = jnp.where(large, code * 2.0 ** -(1 << bit), code)
        cell = jnp.where(large, cell + float(1 << bit), cell)
    tap = jnp.maximum((code * 2.0**124 - 1.0) * OS, 0.0)
    return cell, tap


def bucket(me, vis_ref, own_ref, cells_ref, taps_ref, lhs, rhs, acc):
    first = lax.broadcasted_iota(jnp.int32, (SUB, SUB), 0)
    second = lax.broadcasted_iota(jnp.int32, (SUB, SUB), 1)
    upper = jnp.where(first <= second, 1.0, 0.0).astype(BF16)
    names = lax.broadcasted_iota(jnp.int32, (IMG, CHUNK), 0)
    lines = lax.broadcasted_iota(jnp.int32, (16, CHUNK), 0).astype(F32)
    zero = jnp.zeros((16, CHUNK), BF16)
    one = jnp.ones((16, CHUNK), BF16)
    acc[...] = jnp.zeros_like(acc)

    def step(turn, carry):
        columns = pl.ds(pl.multiple_of(turn * CHUNK, CHUNK), CHUNK)
        offsets = (own_ref[:, columns] + (IMG - me)) & (IMG - 1)
        named = jnp.where(names == offsets, 1.0, 0.0)
        marks = named.astype(BF16)
        ranks = []
        for part in range(CHUNK // SUB):
            span = slice(part * SUB, (part + 1) * SUB)
            counts = dot_nn(marks[:, span], upper) + carry
            ranks.append(jnp.sum(named[:, span] * counts, axis=0, keepdims=True) - 1.0)
            carry = counts[:, SUB - 1 : SUB]
        rank = jnp.concatenate(ranks, axis=1)
        gap = (rank - lines).astype(BF16)
        for block in range(CAP // 16):
            rhs[block * 16 : (block + 1) * 16, :] = jnp.where(gap == block * 16, one, zero)
        codes = encode(cells_ref[:, columns], taps_ref[:, columns])
        features = [
            jnp.broadcast_to(row, (16, CHUNK)).astype(BF16)
            for row in (
                vis_ref[0:1, columns].astype(F32), vis_ref[1:2, columns].astype(F32), codes[0:1], codes[1:2],
            )
        ]
        offset_gap = (offsets.astype(F32) - lines).astype(BF16)
        for block, group in enumerate(ORDER):
            here = offset_gap == group * BLOCK
            for index, feature in enumerate(features):
                row = (block * 4 + index) * 16
                lhs[row : row + 16, :] = jnp.where(here, feature, zero)
        acc[...] += dot_nt(lhs[...], rhs[...])
        return carry

    lax.fori_loop(0, VIS // CHUNK, step, jnp.zeros((IMG, 1), F32))


def make_messages(block, acc, out_ref):
    place = lax.broadcasted_iota(jnp.int32, (8 * 16, 6 * 16), 0)
    origin = lax.broadcasted_iota(jnp.int32, (8 * 16, 6 * 16), 1)
    swap = jnp.where(origin == (place & 7) * 16 + (place >> 3), 1.0, 0.0).astype(BF16)
    found = acc[block * 64 : (block + 1) * 64, :]
    cell, tap = decode(found[32:])
    features = jnp.concatenate([found[:32], cell, tap], axis=0).astype(BF16)
    swapped = dot_nn(swap, features)
    front = swapped[:, :HALF].reshape(16, 8, HALF)
    back = swapped[:, HALF:].reshape(16, 8, HALF)
    out_ref[block * 16 : (block + 1) * 16] = jnp.concatenate([front, back], axis=1).astype(BF16)


def spread(table, cell, tap, lines):
    block = jnp.floor(cell * 0.125)
    low = cell - block * 8.0
    gap = lines - low
    wraps = gap < 0.0
    source = jnp.where(wraps, gap + 8.0, gap).astype(jnp.int32)
    looked = jnp.take_along_axis(table, tap.astype(jnp.int32), axis=1)
    turned = jnp.take_along_axis(looked, source, axis=0)
    return turned, block + jnp.where(wraps, 1.0, 0.0)


def grid_group(arrived, start, table, lhs, rhs):
    lines = lax.broadcasted_iota(jnp.int32, (8, HALF), 0).astype(F32)
    zero = jnp.zeros((16, HALF), BF16)
    for source in range(GROUP):
        message = arrived[start + source].astype(F32)
        for half in range(2):
            slots = message[half * 8 : half * 8 + 8]
            columns = slice((source * 2 + half) * HALF, (source * 2 + half + 1) * HALF)

            def line(index):
                return jnp.broadcast_to(slots[index : index + 1], (8, HALF))

            turned_u, block_u = spread(table, line(2), line(4), lines)
            turned_v, block_v = spread(table, line(3), line(5), lines)
            real, imag = line(0) * turned_u, line(1) * turned_u
            real = jnp.concatenate([real, real], axis=0).astype(BF16)
            imag = jnp.concatenate([imag, imag], axis=0).astype(BF16)
            weight_v = jnp.concatenate([turned_v, turned_v], axis=0).astype(BF16)
            at_u = jnp.concatenate([block_u, block_u - 1.0], axis=0).astype(BF16)
            at_v = jnp.concatenate([block_v, block_v - 1.0], axis=0).astype(BF16)
            for block in range(SUB // 16):
                here = at_u == 2 * block
                lhs[block * 16 : (block + 1) * 16, columns] = jnp.where(here, real, zero)
                lhs[SUB + block * 16 : SUB + (block + 1) * 16, columns] = jnp.where(here, imag, zero)
                rhs[block * 16 : (block + 1) * 16, columns] = jnp.where(at_v == 2 * block, weight_v, zero)


def main_kernel(
    vis_hbm, own_hbm, cells_hbm, taps_hbm, table_hbm, rows_hbm, cols_hbm, v_hbm, u_hbm, last_hbm, twist_hbm, out_ref,
    vis_ref, own_ref, cells_ref, taps_ref, table_ref, rows_ref, cols_ref, v_ref, u_ref, last_ref, twist_ref,
    acc, lhs, rhs, lhs_grid, rhs_grid, sent, arrived, grid, cross_out, cross_in, out_two, in_two, out_three, in_three,
    final_table, factor, load_sem, send_sem, recv_sem, cross_sem, far_send, far_recv, own_sem,
):
    me, chan = lax.axis_index("img"), lax.axis_index("chan")
    loads = [
        pltpu.make_async_copy(source, target, load_sem.at[index])
        for index, (source, target) in enumerate(
            [
                (vis_hbm, vis_ref), (own_hbm, own_ref), (cells_hbm, cells_ref), (taps_hbm, taps_ref),
                (table_hbm, table_ref), (rows_hbm, rows_ref), (cols_hbm, cols_ref), (twist_hbm.at[me], twist_ref),
                (last_hbm, last_ref), (v_hbm, v_ref), (u_hbm, u_ref),
            ]
        )
    ]
    for load in loads:
        load.start()
    barrier = pltpu.get_barrier_semaphore()

    def greet(step, count):
        pl.semaphore_signal(barrier, inc=1, device_id=(lax.rem(me + step, IMG), chan), device_id_type=MESH)
        return count

    lax.fori_loop(1, IMG, greet, 0)
    pl.semaphore_signal(barrier, inc=1, device_id=(me, 1 - chan), device_id_type=MESH)

    for load in loads[:4]:
        load.wait()
    bucket(me, vis_ref, own_ref, cells_ref, taps_ref, lhs, rhs, acc)

    def send_block(block):
        group = ORDER[block]

        def send(step, count):
            peer = lax.rem(me + group * BLOCK + step, IMG)
            pltpu.make_async_remote_copy(
                src_ref=sent.at[block * BLOCK + step], dst_ref=arrived.at[block * BLOCK + step],
                send_sem=send_sem, recv_sem=recv_sem.at[block], device_id=(peer, chan), device_id_type=MESH,
            ).start()
            return count

        lax.fori_loop(0 if group else 1, BLOCK, send, 0)

    self_block = ORDER.index(0)
    own = pltpu.make_async_copy(sent.at[self_block * BLOCK], arrived.at[self_block * BLOCK], own_sem.at[0])
    make_messages(0, acc, sent)
    pl.semaphore_wait(barrier, IMG)
    own.start()
    send_block(0)
    for block in range(1, 8):
        make_messages(block, acc, sent)
        send_block(block)

    for load in loads[4:]:
        load.wait()
    cosine, sine = twist_ref[0:1, :], twist_ref[1:2, :]
    base_cos, base_sin = last_ref[0], last_ref[1]
    for part, value in enumerate((base_cos * cosine - base_sin * sine, base_sin * cosine + base_cos * sine)):
        high, low = split_pair(value)
        final_table[part * SUB : (part + 1) * SUB, :SUB] = high
        final_table[part * SUB : (part + 1) * SUB, SUB:] = low
    scale = 1.0 / math.sqrt(SUB * IMG * SUB)
    for block in range(2):
        rows = slice(block * HALF, (block + 1) * HALF)
        column = jnp.transpose(jnp.broadcast_to(rows_ref[:, rows], (HALF, HALF)))
        factor[rows, :] = column * cols_ref[...] * scale

    grid[...] = jnp.zeros_like(grid)
    table = table_ref[...].astype(F32)
    own.wait()

    def wait_block(block):
        def wait_count(count):
            span = pl.ds(0, count)
            pltpu.make_async_remote_copy(
                src_ref=sent.at[span], dst_ref=arrived.at[span], send_sem=send_sem, recv_sem=recv_sem.at[block],
                device_id=(me, 1 - chan), device_id_type=MESH,
            ).wait_recv()

        @pl.when(block == self_block)
        def _():
            wait_count(BLOCK - 1)

        @pl.when(block != self_block)
        def _():
            wait_count(BLOCK)

    def grid_step(group, count):
        for block in range(GROUP // BLOCK):
            wait_block(group * (GROUP // BLOCK) + block)
        grid_group(arrived, group * GROUP, table, lhs_grid, rhs_grid)
        grid[...] += dot_nt(lhs_grid[...], rhs_grid[...])
        return count

    lax.fori_loop(0, IMG // GROUP, grid_step, 0)

    both = jnp.concatenate([grid[:SUB, :], grid[SUB:, :]], axis=1)
    high, low = split_pair(both)
    pieces = jnp.concatenate([high, high, low], axis=1)

    cross_out[...] = dot_nn(pieces, v_ref[1 - chan])
    cross = pltpu.make_async_remote_copy(
        src_ref=cross_out, dst_ref=cross_in, send_sem=cross_sem.at[0], recv_sem=cross_sem.at[1],
        device_id=(me, 1 - chan), device_id_type=MESH,
    )
    cross.start()
    mine = dot_nn(pieces, v_ref[chan])
    cross.wait_recv()
    out_two[...] = (mine + cross_in[...]).reshape(IMG, 2, SUB).astype(BF16)

    def complex_dot(table, columns):
        product = dot_nn(table, jnp.concatenate([columns, columns], axis=0))
        real = product[:SUB, :HALF] - product[SUB:, HALF:]
        imag = product[SUB:, :HALF] + product[:SUB, HALF:]
        return real, imag

    def exchange(source, target, phase):
        keep = pltpu.make_async_copy(source.at[me], target.at[me], own_sem.at[1 + phase])
        keep.start()

        def send(step, count):
            peer = lax.rem(me + FAR + step, IMG)
            pltpu.make_async_remote_copy(
                src_ref=source.at[peer], dst_ref=target.at[me], send_sem=far_send.at[phase],
                recv_sem=far_recv.at[phase], device_id=(peer, chan), device_id_type=MESH,
            ).start()
            return count

        lax.fori_loop(0, IMG - FAR, send, 0)
        lax.fori_loop(IMG - FAR + 1, IMG, send, 0)
        keep.wait()
        span = pl.ds(0, IMG - 1)
        return pltpu.make_async_remote_copy(
            src_ref=source.at[span], dst_ref=target.at[span], send_sem=far_send.at[phase],
            recv_sem=far_recv.at[phase], device_id=(me, 1 - chan), device_id_type=MESH,
        )

    second = exchange(out_two, in_two, 0)
    second.wait_recv()
    real, imag = complex_dot(u_ref[...], in_two[...].reshape(SUB, SUB))
    out_three[...] = jnp.concatenate([real, imag], axis=1).reshape(IMG, 2, SUB).astype(BF16)
    third = exchange(out_three, in_three, 1)
    third.wait_recv()
    real, imag = complex_dot(final_table[...], in_three[...].reshape(SUB, SUB))
    out_ref[0] = real * factor[...]
    out_ref[1] = imag * factor[...]

    span = pl.ds(0, IMG - 1)
    pltpu.make_async_remote_copy(
        src_ref=sent.at[span], dst_ref=arrived.at[span], send_sem=send_sem, recv_sem=recv_sem.at[0],
        device_id=(me, 1 - chan), device_id_type=MESH,
    ).wait_send()
    cross.wait_send()
    second.wait_send()
    third.wait_send()


def body(visibilities, owner, cells, taps, kernel, taper_rows, taper_cols):
    v_tables, u_table, last_tables, twists = host_tables()
    return pl.pallas_call(
        main_kernel,
        out_shape=jax.ShapeDtypeStruct((2, SUB, HALF), F32),
        in_specs=[pl.BlockSpec(memory_space=pltpu.HBM)] * 11,
        out_specs=pl.BlockSpec(memory_space=pltpu.VMEM),
        scratch_shapes=[
            pltpu.VMEM((2, VIS), BF16),
            pltpu.VMEM((1, VIS), jnp.int32),
            pltpu.VMEM((2, VIS), jnp.int32),
            pltpu.VMEM((2, VIS), jnp.int32),
            pltpu.VMEM((TAPS, OS), BF16),
            pltpu.VMEM((1, SUB), F32),
            pltpu.VMEM((1, HALF), F32),
            pltpu.VMEM(v_tables.shape, BF16),
            pltpu.VMEM(u_table.shape, BF16),
            pltpu.VMEM(last_tables.shape, F32),
            pltpu.VMEM(twists.shape[1:], F32),
            pltpu.VMEM((4 * IMG, CAP), F32),
            pltpu.VMEM((4 * IMG, CHUNK), BF16),
            pltpu.VMEM((CAP, CHUNK), BF16),
            pltpu.VMEM((2 * SUB, GROUP * CAP), BF16),
            pltpu.VMEM((SUB, GROUP * CAP), BF16),
            pltpu.VMEM((IMG, 16, HALF), BF16),
            pltpu.VMEM((IMG, 16, HALF), BF16),
            pltpu.VMEM((2 * SUB, SUB), F32),
            pltpu.VMEM((SUB, SUB), F32),
            pltpu.VMEM((SUB, SUB), F32),
            pltpu.VMEM((IMG, 2, SUB), BF16),
            pltpu.VMEM((IMG, 2, SUB), BF16),
            pltpu.VMEM((IMG, 2, SUB), BF16),
            pltpu.VMEM((IMG, 2, SUB), BF16),
            pltpu.VMEM((2 * SUB, 2 * SUB), BF16),
            pltpu.VMEM((SUB, HALF), F32),
            pltpu.SemaphoreType.DMA((11,)),
            pltpu.SemaphoreType.DMA(()),
            pltpu.SemaphoreType.DMA((IMG // BLOCK,)),
            pltpu.SemaphoreType.DMA((2,)),
            pltpu.SemaphoreType.DMA((2,)),
            pltpu.SemaphoreType.DMA((2,)),
            pltpu.SemaphoreType.DMA((3,)),
        ],
        compiler_params=pltpu.CompilerParams(
            collective_id=0, has_side_effects=True, vmem_limit_bytes=60 * 1024 * 1024
        ),
        name="gridding",
    )(
        visibilities[0], owner.reshape(1, VIS), cells[0], taps[0], kernel.T,
        taper_rows.reshape(1, SUB), taper_cols.reshape(1, HALF),
        jnp.asarray(v_tables), jnp.asarray(u_table), jnp.asarray(last_tables), jnp.asarray(twists),
    )


def solution(mesh):
    return jax.shard_map(
        body,
        mesh=mesh,
        in_specs=(
            P("chan", None, "img"),
            P("chan", "img", None),
            P("chan", None, "img"),
            P("chan", None, "img"),
            P(),
            P("img"),
            P("chan"),
        ),
        out_specs=P(None, "img", "chan"),
        check_vma=False,
    )
```

```python
import functools
import math

import jax
import jax.numpy as jnp
import numpy as np
from jax import lax
from jax.experimental import pallas as pl
from jax.experimental.pallas import tpu as pltpu
from jax.sharding import PartitionSpec as P

SUB = 256
TAPS = 8
OS = 128
IMG = 128
HALF = 128
CAP = 256
VIS = 16384
CHUNK = 8192
BLOCK = 16
GROUP = 32
ORDER = (0, 7, 1, 6, 2, 5, 3, 4)
F32 = jnp.float32
BF16 = jnp.bfloat16
MESH = pl.DeviceIdType.MESH


def hops(offset):
    return sum(min(step, size - step) for step, size in zip(offset, TORUS))


TORUS = (4, 4, 8)
FAR_FIRST = sorted(list(np.ndindex(TORUS))[1:], key=hops, reverse=True)


def split_table(table):
    high = table.astype(np.float32).astype(jnp.bfloat16)
    low = (table - high.astype(np.float64)).astype(np.float32).astype(jnp.bfloat16)
    return high, low


def reversed_bits(count):
    bits = count.bit_length() - 1
    positions = np.arange(count)
    order = np.zeros(count, np.int64)
    for bit in range(bits):
        order |= (positions >> bit & 1) << bits - 1 - bit
    return order


@functools.lru_cache(maxsize=None)
def host_tables():
    points = np.arange(SUB)
    angle = 2 * np.pi * (points[:, None] * points[None, :] % SUB) / SUB
    cosine, sine = np.cos(angle), np.sin(angle)
    halves = []
    for start in (0, HALF):
        half_cos, half_sin = cosine[:, start : start + HALF], sine[:, start : start + HALF]
        high, low = split_table(np.block([[half_cos, half_sin], [-half_sin, half_cos]]))
        halves.append(np.concatenate([high, low, high], axis=0))
    v_tables = np.stack(halves)
    order = reversed_bits(IMG)
    turn = 2 * np.pi * (order[:, None] * np.arange(IMG)[None, :] % IMG) / IMG
    each = np.eye(2)
    high, low = split_table(np.concatenate([np.kron(np.cos(turn), each), np.kron(np.sin(turn), each)], axis=0))
    u_table = np.concatenate([high, low], axis=1)
    last_tables = np.stack([cosine, sine]).astype(np.float32)
    twist = 2 * np.pi * (order[:, None] * points[None, :]) / (IMG * SUB)
    twists = np.stack([np.cos(twist), np.sin(twist)], 1).astype(np.float32)
    return v_tables, u_table, last_tables, twists


def dot_nt(left, right):
    return lax.dot_general(left, right, (((1,), (1,)), ((), ())), preferred_element_type=F32)


def dot_nn(left, right):
    return lax.dot_general(left, right, (((1,), (0,)), ((), ())), preferred_element_type=F32)


def split_pair(value):
    high = value.astype(BF16)
    low = (value - high.astype(F32)).astype(BF16)
    return high, low


def encode(cell, tap):
    code = jnp.full(cell.shape, 2.0**-124, F32)
    for bit in range(7):
        code = jnp.where((cell >> bit & 1) == 1, code * 2.0 ** (1 << bit), code)
    code = jnp.where(cell >> 7 == 1, code * 2.0**64 * 2.0**64, code)
    return code * (1.0 + tap.astype(F32) * (1.0 / OS))


def decode(code):
    cell = jnp.zeros(code.shape, F32)
    large = code >= 2.0**4
    code = jnp.where(large, code * 2.0**-64 * 2.0**-64, code)
    cell = jnp.where(large, cell + 128.0, cell)
    for bit in range(6, -1, -1):
        large = code >= 2.0 ** ((1 << bit) - 124)
        code = jnp.where(large, code * 2.0 ** -(1 << bit), code)
        cell = jnp.where(large, cell + float(1 << bit), cell)
    tap = jnp.maximum((code * 2.0**124 - 1.0) * OS, 0.0)
    return cell, tap


def bucket(me, vis_ref, own_ref, cells_ref, taps_ref, lhs, rhs, acc):
    first = lax.broadcasted_iota(jnp.int32, (SUB, SUB), 0)
    second = lax.broadcasted_iota(jnp.int32, (SUB, SUB), 1)
    upper = jnp.where(first <= second, 1.0, 0.0).astype(BF16)
    lines = lax.broadcasted_iota(jnp.int32, (16, CHUNK), 0).astype(F32)
    zero = jnp.zeros((16, CHUNK), BF16)
    one = jnp.ones((16, CHUNK), BF16)
    acc[...] = jnp.zeros_like(acc)

    def step(turn, carry):
        columns = slice(turn * CHUNK, (turn + 1) * CHUNK)
        offsets = (own_ref[:, columns] + (IMG - me)) & (IMG - 1)
        codes = encode(cells_ref[:, columns], taps_ref[:, columns])
        features = [
            jnp.broadcast_to(row, (16, CHUNK)).astype(BF16)
            for row in (
                vis_ref[0:1, columns].astype(F32), vis_ref[1:2, columns].astype(F32), codes[0:1], codes[1:2],
            )
        ]
        offset_gap = (offsets.astype(F32) - lines).astype(BF16)
        marks = []
        for block, group in enumerate(ORDER):
            here = offset_gap == group * BLOCK
            marks.append(jnp.where(here, one, zero))
            for index, feature in enumerate(features):
                row = (block * 4 + index) * 16
                lhs[row : row + 16, :] = jnp.where(here, feature, zero)
        marks = jnp.concatenate(marks, axis=0)
        parts = [marks[:, part * SUB : (part + 1) * SUB] for part in range(CHUNK // SUB)]
        within = dot_nn(jnp.concatenate(parts, axis=0), upper)
        ranks = []
        for index, part in enumerate(parts):
            counts = within[index * IMG : (index + 1) * IMG] + carry
            found = part * counts.astype(BF16)
            while found.shape[0] > 16:
                found = found[: found.shape[0] // 2] + found[found.shape[0] // 2 :]
            ranks.append(jnp.sum(found.astype(F32), axis=0, keepdims=True) - 1.0)
            carry = counts[:, SUB - 1 : SUB]
        rank = jnp.concatenate(ranks, axis=1)
        gap = (rank - lines).astype(BF16)
        for block in range(CAP // 16):
            rhs[block * 16 : (block + 1) * 16, :] = jnp.where(gap == block * 16, one, zero)
        acc[...] += dot_nt(lhs[...], rhs[...])
        return carry

    carry = jnp.zeros((IMG, 1), F32)
    for turn in range(VIS // CHUNK):
        carry = step(turn, carry)


def make_messages(block, acc, out_ref):
    place = lax.broadcasted_iota(jnp.int32, (8 * 16, 6 * 16), 0)
    origin = lax.broadcasted_iota(jnp.int32, (8 * 16, 6 * 16), 1)
    swap = jnp.where(origin == (place & 7) * 16 + (place >> 3), 1.0, 0.0).astype(BF16)
    found = acc[block * 64 : (block + 1) * 64, :]
    cell, tap = decode(found[32:])
    features = jnp.concatenate([found[:32], cell, tap], axis=0).astype(BF16)
    swapped = dot_nn(swap, features)
    front = swapped[:, :HALF].reshape(16, 8, HALF)
    back = swapped[:, HALF:].reshape(16, 8, HALF)
    out_ref[block * 16 : (block + 1) * 16] = jnp.concatenate([front, back], axis=1).astype(BF16)


def spread(table, cell, tap, lines):
    block = jnp.floor(cell * 0.125)
    low = cell - block * 8.0
    gap = lines - low
    wraps = gap < 0.0
    source = jnp.where(wraps, gap + 8.0, gap).astype(jnp.int32)
    looked = jnp.take_along_axis(table, tap.astype(jnp.int32), axis=1)
    turned = jnp.take_along_axis(looked, source, axis=0)
    return turned, block + jnp.where(wraps, 1.0, 0.0)


def grid_group(arrived, start, table, lhs, rhs):
    lines = lax.broadcasted_iota(jnp.int32, (8, HALF), 0).astype(F32)
    zero = jnp.zeros((16, HALF), BF16)
    for source in range(GROUP):
        message = arrived[start + source].astype(F32)
        for half in range(2):
            slots = message[half * 8 : half * 8 + 8]
            columns = slice((source * 2 + half) * HALF, (source * 2 + half + 1) * HALF)

            def line(index):
                return jnp.broadcast_to(slots[index : index + 1], (8, HALF))

            turned_u, block_u = spread(table, line(2), line(4), lines)
            turned_v, block_v = spread(table, line(3), line(5), lines)
            real, imag = line(0) * turned_u, line(1) * turned_u
            real = jnp.concatenate([real, real], axis=0).astype(BF16)
            imag = jnp.concatenate([imag, imag], axis=0).astype(BF16)
            weight_v = jnp.concatenate([turned_v, turned_v], axis=0).astype(BF16)
            at_u = jnp.concatenate([block_u, block_u - 1.0], axis=0).astype(BF16)
            at_v = jnp.concatenate([block_v, block_v - 1.0], axis=0).astype(BF16)
            for block in range(SUB // 16):
                here = at_u == 2 * block
                lhs[block * 16 : (block + 1) * 16, columns] = jnp.where(here, real, zero)
                lhs[SUB + block * 16 : SUB + (block + 1) * 16, columns] = jnp.where(here, imag, zero)
                rhs[block * 16 : (block + 1) * 16, columns] = jnp.where(at_v == 2 * block, weight_v, zero)


def main_kernel(
    vis_hbm, own_hbm, cells_hbm, taps_hbm, table_hbm, rows_hbm, cols_hbm, v_hbm, u_hbm, last_hbm, twist_hbm, out_ref,
    vis_ref, own_ref, cells_ref, taps_ref, table_ref, rows_ref, cols_ref, v_ref, u_ref, last_ref, twist_ref,
    acc, lhs, rhs, lhs_grid, rhs_grid, sent, arrived, grid, cross_out, cross_in, out_two, in_two, out_three, in_three,
    final_table, factor, load_sem, send_sem, recv_sem, cross_sem, far_send, far_recv, own_sem,
):
    me, chan = lax.axis_index("img"), lax.axis_index("chan")
    loads = [
        pltpu.make_async_copy(source, target, load_sem.at[index])
        for index, (source, target) in enumerate(
            [
                (vis_hbm, vis_ref), (own_hbm, own_ref), (cells_hbm, cells_ref), (taps_hbm, taps_ref),
                (table_hbm, table_ref), (rows_hbm, rows_ref), (cols_hbm, cols_ref), (twist_hbm.at[me], twist_ref),
                (last_hbm, last_ref), (v_hbm, v_ref), (u_hbm, u_ref),
            ]
        )
    ]
    for load in loads[:4]:
        load.start()
    barrier = pltpu.get_barrier_semaphore()

    def greet(step):
        pl.semaphore_signal(barrier, inc=1, device_id=((me + step) & (IMG - 1), chan), device_id_type=MESH)

    pl.semaphore_signal(barrier, inc=1, device_id=(me, 1 - chan), device_id_type=MESH)
    for step in range(1, IMG // 2):
        greet(step)
    for load in loads[:4]:
        load.wait()
    for load in loads[4:]:
        load.start()
    for step in range(IMG // 2, IMG):
        greet(step)
    bucket(me, vis_ref, own_ref, cells_ref, taps_ref, lhs, rhs, acc)

    def send_block(block):
        for step in range(BLOCK):
            offset = ORDER[block] * BLOCK + step
            if offset:
                pltpu.make_async_remote_copy(
                    src_ref=sent.at[block * BLOCK + step], dst_ref=arrived.at[block * BLOCK + step],
                    send_sem=send_sem, recv_sem=recv_sem.at[block],
                    device_id=((me + offset) & (IMG - 1), chan), device_id_type=MESH,
                ).start()

    self_block = ORDER.index(0)
    own = pltpu.make_async_copy(sent.at[self_block * BLOCK], arrived.at[self_block * BLOCK], own_sem.at[0])
    make_messages(0, acc, sent)
    pl.semaphore_wait(barrier, IMG)
    own.start()
    send_block(0)
    for block in range(1, 8):
        make_messages(block, acc, sent)
        send_block(block)

    for load in loads[4:]:
        load.wait()
    grid[...] = jnp.zeros_like(grid)
    table = table_ref[...].astype(F32)
    own.wait()

    def wait_block(block):
        def wait_count(count):
            span = pl.ds(0, count)
            pltpu.make_async_remote_copy(
                src_ref=sent.at[span], dst_ref=arrived.at[span], send_sem=send_sem, recv_sem=recv_sem.at[block],
                device_id=(me, 1 - chan), device_id_type=MESH,
            ).wait_recv()

        @pl.when(block == self_block)
        def _():
            wait_count(BLOCK - 1)

        @pl.when(block != self_block)
        def _():
            wait_count(BLOCK)

    def grid_step(group, count):
        for block in range(GROUP // BLOCK):
            wait_block(group * (GROUP // BLOCK) + block)
        grid_group(arrived, group * GROUP, table, lhs_grid, rhs_grid)
        grid[...] += dot_nt(lhs_grid[...], rhs_grid[...])
        return count

    lax.fori_loop(0, IMG // GROUP, grid_step, 0)

    both = jnp.concatenate([grid[:SUB, :], grid[SUB:, :]], axis=1)
    high, low = split_pair(both)
    pieces = jnp.concatenate([high, high, low], axis=1)

    cross_out[...] = dot_nn(pieces, v_ref[1 - chan])
    cross = pltpu.make_async_remote_copy(
        src_ref=cross_out, dst_ref=cross_in, send_sem=cross_sem.at[0], recv_sem=cross_sem.at[1],
        device_id=(me, 1 - chan), device_id_type=MESH,
    )
    cross.start()
    mine = dot_nn(pieces, v_ref[chan])
    cross.wait_recv()
    out_two[...] = (mine + cross_in[...]).reshape(IMG, 2, SUB).astype(BF16)

    def complex_dot(table, columns):
        product = dot_nn(table, jnp.concatenate([columns, columns], axis=0))
        real = product[:SUB, :HALF] - product[SUB:, HALF:]
        imag = product[SUB:, :HALF] + product[:SUB, HALF:]
        return real, imag

    place_y, place_x, place_z = me >> 5, me >> 3 & 3, me & 7
    rows_y = [(place_y + step & 3) * 32 for step in range(TORUS[0])]
    rows_x = [(place_x + step & 3) * 8 for step in range(TORUS[1])]
    rows_z = [place_z + step & 7 for step in range(TORUS[2])]

    def exchange(source, target, phase):
        keep = pltpu.make_async_copy(source.at[me], target.at[me], own_sem.at[1 + phase])
        keep.start()

        for far_y, far_x, far_z in FAR_FIRST:
            peer = rows_y[far_y] + rows_x[far_x] + rows_z[far_z]
            pltpu.make_async_remote_copy(
                src_ref=source.at[peer], dst_ref=target.at[me], send_sem=far_send.at[phase],
                recv_sem=far_recv.at[phase], device_id=(peer, chan), device_id_type=MESH,
            ).start()
        keep.wait()
        span = pl.ds(0, IMG - 1)
        return pltpu.make_async_remote_copy(
            src_ref=source.at[span], dst_ref=target.at[span], send_sem=far_send.at[phase],
            recv_sem=far_recv.at[phase], device_id=(me, 1 - chan), device_id_type=MESH,
        )

    second = exchange(out_two, in_two, 0)
    cosine, sine = twist_ref[0:1, :], twist_ref[1:2, :]
    base_cos, base_sin = last_ref[0], last_ref[1]
    for part, value in enumerate((base_cos * cosine - base_sin * sine, base_sin * cosine + base_cos * sine)):
        high, low = split_pair(value)
        final_table[part * SUB : (part + 1) * SUB, :SUB] = high
        final_table[part * SUB : (part + 1) * SUB, SUB:] = low
    scale = 1.0 / math.sqrt(SUB * IMG * SUB)
    for block in range(2):
        rows = slice(block * HALF, (block + 1) * HALF)
        column = jnp.transpose(jnp.broadcast_to(rows_ref[:, rows], (HALF, HALF)))
        factor[rows, :] = column * cols_ref[...] * scale
    second.wait_recv()
    real, imag = complex_dot(u_ref[...], in_two[...].reshape(SUB, SUB))
    out_three[...] = jnp.concatenate([real, imag], axis=1).reshape(IMG, 2, SUB).astype(BF16)
    third = exchange(out_three, in_three, 1)
    third.wait_recv()
    real, imag = complex_dot(final_table[...], in_three[...].reshape(SUB, SUB))
    out_ref[0] = real * factor[...]
    out_ref[1] = imag * factor[...]

    span = pl.ds(0, IMG - 1)
    pltpu.make_async_remote_copy(
        src_ref=sent.at[span], dst_ref=arrived.at[span], send_sem=send_sem, recv_sem=recv_sem.at[0],
        device_id=(me, 1 - chan), device_id_type=MESH,
    ).wait_send()
    cross.wait_send()
    second.wait_send()
    third.wait_send()


def body(visibilities, owner, cells, taps, kernel, taper_rows, taper_cols):
    v_tables, u_table, last_tables, twists = host_tables()
    return pl.pallas_call(
        main_kernel,
        out_shape=jax.ShapeDtypeStruct((2, SUB, HALF), F32),
        in_specs=[pl.BlockSpec(memory_space=pltpu.HBM)] * 11,
        out_specs=pl.BlockSpec(memory_space=pltpu.VMEM),
        scratch_shapes=[
            pltpu.VMEM((2, VIS), BF16),
            pltpu.VMEM((1, VIS), jnp.int32),
            pltpu.VMEM((2, VIS), jnp.int32),
            pltpu.VMEM((2, VIS), jnp.int32),
            pltpu.VMEM((TAPS, OS), BF16),
            pltpu.VMEM((1, SUB), F32),
            pltpu.VMEM((1, HALF), F32),
            pltpu.VMEM(v_tables.shape, BF16),
            pltpu.VMEM(u_table.shape, BF16),
            pltpu.VMEM(last_tables.shape, F32),
            pltpu.VMEM(twists.shape[1:], F32),
            pltpu.VMEM((4 * IMG, CAP), F32),
            pltpu.VMEM((4 * IMG, CHUNK), BF16),
            pltpu.VMEM((CAP, CHUNK), BF16),
            pltpu.VMEM((2 * SUB, GROUP * CAP), BF16),
            pltpu.VMEM((SUB, GROUP * CAP), BF16),
            pltpu.VMEM((IMG, 16, HALF), BF16),
            pltpu.VMEM((IMG, 16, HALF), BF16),
            pltpu.VMEM((2 * SUB, SUB), F32),
            pltpu.VMEM((SUB, SUB), F32),
            pltpu.VMEM((SUB, SUB), F32),
            pltpu.VMEM((IMG, 2, SUB), BF16),
            pltpu.VMEM((IMG, 2, SUB), BF16),
            pltpu.VMEM((IMG, 2, SUB), BF16),
            pltpu.VMEM((IMG, 2, SUB), BF16),
            pltpu.VMEM((2 * SUB, 2 * SUB), BF16),
            pltpu.VMEM((SUB, HALF), F32),
            pltpu.SemaphoreType.DMA((11,)),
            pltpu.SemaphoreType.DMA(()),
            pltpu.SemaphoreType.DMA((IMG // BLOCK,)),
            pltpu.SemaphoreType.DMA((2,)),
            pltpu.SemaphoreType.DMA((2,)),
            pltpu.SemaphoreType.DMA((2,)),
            pltpu.SemaphoreType.DMA((3,)),
        ],
        compiler_params=pltpu.CompilerParams(
            collective_id=0, has_side_effects=True, vmem_limit_bytes=60 * 1024 * 1024
        ),
        name="gridding",
    )(
        visibilities[0], owner.reshape(1, VIS), cells[0], taps[0], kernel.T,
        taper_rows.reshape(1, SUB), taper_cols.reshape(1, HALF),
        jnp.asarray(v_tables), jnp.asarray(u_table), jnp.asarray(last_tables), jnp.asarray(twists),
    )


def solution(mesh):
    return jax.shard_map(
        body,
        mesh=mesh,
        in_specs=(
            P("chan", None, "img"),
            P("chan", "img", None),
            P("chan", None, "img"),
            P("chan", None, "img"),
            P(),
            P("img"),
            P("chan"),
        ),
        out_specs=P(None, "img", "chan"),
        check_vma=False,
    )
```

```python
import functools
import math

import jax
import jax.numpy as jnp
import numpy as np
from jax import lax
from jax.experimental import pallas as pl
from jax.experimental.pallas import tpu as pltpu
from jax.sharding import PartitionSpec as P

SUB = 256
TAPS = 8
OS = 128
IMG = 128
HALF = 128
CAP = 256
VIS = 16384
CHUNK = VIS
BLOCK = 16
GROUP = 32
ORDER = (0, 7, 1, 6, 2, 5, 3, 4)
F32 = jnp.float32
BF16 = jnp.bfloat16
MESH = pl.DeviceIdType.MESH


def hops(offset):
    return sum(min(step, size - step) for step, size in zip(offset, TORUS))


TORUS = (4, 4, 8)
FAR_FIRST = sorted(list(np.ndindex(TORUS))[1:], key=hops, reverse=True)


def split_table(table):
    high = table.astype(np.float32).astype(jnp.bfloat16)
    low = (table - high.astype(np.float64)).astype(np.float32).astype(jnp.bfloat16)
    return high, low


def reversed_bits(count):
    bits = count.bit_length() - 1
    positions = np.arange(count)
    order = np.zeros(count, np.int64)
    for bit in range(bits):
        order |= (positions >> bit & 1) << bits - 1 - bit
    return order


@functools.lru_cache(maxsize=None)
def host_tables():
    points = np.arange(SUB)
    angle = 2 * np.pi * (points[:, None] * points[None, :] % SUB) / SUB
    cosine, sine = np.cos(angle), np.sin(angle)
    halves = []
    for start in (0, HALF):
        half_cos, half_sin = cosine[:, start : start + HALF], sine[:, start : start + HALF]
        high, low = split_table(np.block([[half_cos, half_sin], [-half_sin, half_cos]]))
        halves.append(np.concatenate([high, low, high], axis=0))
    v_tables = np.stack(halves)
    order = reversed_bits(IMG)
    turn = 2 * np.pi * (order[:, None] * np.arange(IMG)[None, :] % IMG) / IMG
    each = np.eye(2)
    high, low = split_table(np.concatenate([np.kron(np.cos(turn), each), np.kron(np.sin(turn), each)], axis=0))
    u_table = np.concatenate([high, low], axis=1)
    last_tables = np.stack([cosine, sine]).astype(np.float32)
    twist = 2 * np.pi * (order[:, None] * points[None, :]) / (IMG * SUB)
    twists = np.stack([np.cos(twist), np.sin(twist)], 1).astype(np.float32)
    return v_tables, u_table, last_tables, twists


def dot_nt(left, right):
    return lax.dot_general(left, right, (((1,), (1,)), ((), ())), preferred_element_type=F32)


def dot_nn(left, right):
    return lax.dot_general(left, right, (((1,), (0,)), ((), ())), preferred_element_type=F32)


def split_pair(value):
    high = value.astype(BF16)
    low = (value - high.astype(F32)).astype(BF16)
    return high, low


def encode(cell, tap):
    code = jnp.full(cell.shape, 2.0**-124, F32)
    for bit in range(7):
        code = jnp.where((cell >> bit & 1) == 1, code * 2.0 ** (1 << bit), code)
    code = jnp.where(cell >> 7 == 1, code * 2.0**64 * 2.0**64, code)
    return code * (1.0 + tap.astype(F32) * (1.0 / OS))


def decode(code):
    cell = jnp.zeros(code.shape, F32)
    large = code >= 2.0**4
    code = jnp.where(large, code * 2.0**-64 * 2.0**-64, code)
    cell = jnp.where(large, cell + 128.0, cell)
    for bit in range(6, -1, -1):
        large = code >= 2.0 ** ((1 << bit) - 124)
        code = jnp.where(large, code * 2.0 ** -(1 << bit), code)
        cell = jnp.where(large, cell + float(1 << bit), cell)
    tap = jnp.maximum((code * 2.0**124 - 1.0) * OS, 0.0)
    return cell, tap


def bucket(me, vis_ref, own_ref, cells_ref, taps_ref, lhs, rhs, acc):
    first = lax.broadcasted_iota(jnp.int32, (SUB, SUB), 0)
    second = lax.broadcasted_iota(jnp.int32, (SUB, SUB), 1)
    upper = jnp.where(first <= second, 1.0, 0.0).astype(BF16)
    lines = lax.broadcasted_iota(jnp.int32, (16, CHUNK), 0).astype(F32)
    zero = jnp.zeros((16, CHUNK), BF16)
    one = jnp.ones((16, CHUNK), BF16)
    acc[...] = jnp.zeros_like(acc)

    def step(turn, carry):
        columns = slice(turn * CHUNK, (turn + 1) * CHUNK)
        offsets = (own_ref[:, columns] + (IMG - me)) & (IMG - 1)
        codes = encode(cells_ref[:, columns], taps_ref[:, columns])
        features = [
            jnp.broadcast_to(row, (16, CHUNK)).astype(BF16)
            for row in (
                vis_ref[0:1, columns].astype(F32), vis_ref[1:2, columns].astype(F32), codes[0:1], codes[1:2],
            )
        ]
        offset_gap = (offsets.astype(F32) - lines).astype(BF16)
        marks = []
        for block, group in enumerate(ORDER):
            here = offset_gap == group * BLOCK
            marks.append(jnp.where(here, one, zero))
            for index, feature in enumerate(features):
                row = (block * 4 + index) * 16
                lhs[row : row + 16, :] = jnp.where(here, feature, zero)
        marks = jnp.concatenate(marks, axis=0)
        parts = [marks[:, part * SUB : (part + 1) * SUB] for part in range(CHUNK // SUB)]
        within = dot_nn(jnp.concatenate(parts, axis=0), upper)
        ranks = []
        for index, part in enumerate(parts):
            counts = within[index * IMG : (index + 1) * IMG] + carry
            found = part * counts.astype(BF16)
            while found.shape[0] > 16:
                found = found[: found.shape[0] // 2] + found[found.shape[0] // 2 :]
            ranks.append(jnp.sum(found.astype(F32), axis=0, keepdims=True) - 1.0)
            carry = counts[:, SUB - 1 : SUB]
        rank = jnp.concatenate(ranks, axis=1)
        gap = (rank - lines).astype(BF16)
        for block in range(CAP // 16):
            rhs[block * 16 : (block + 1) * 16, :] = jnp.where(gap == block * 16, one, zero)
        acc[...] += dot_nt(lhs[...], rhs[...])
        return carry

    carry = jnp.zeros((IMG, 1), F32)
    for turn in range(VIS // CHUNK):
        carry = step(turn, carry)


def make_messages(block, acc, out_ref):
    place = lax.broadcasted_iota(jnp.int32, (8 * 16, 6 * 16), 0)
    origin = lax.broadcasted_iota(jnp.int32, (8 * 16, 6 * 16), 1)
    swap = jnp.where(origin == (place & 7) * 16 + (place >> 3), 1.0, 0.0).astype(BF16)
    found = acc[block * 64 : (block + 1) * 64, :]
    cell, tap = decode(found[32:])
    features = jnp.concatenate([found[:32], cell, tap], axis=0).astype(BF16)
    swapped = dot_nn(swap, features)
    front = swapped[:, :HALF].reshape(16, 8, HALF)
    back = swapped[:, HALF:].reshape(16, 8, HALF)
    out_ref[block * 16 : (block + 1) * 16] = jnp.concatenate([front, back], axis=1).astype(BF16)


def spread(table, cell, tap, lines):
    block = jnp.floor(cell * 0.125)
    low = cell - block * 8.0
    gap = lines - low
    wraps = gap < 0.0
    source = jnp.where(wraps, gap + 8.0, gap).astype(jnp.int32)
    looked = jnp.take_along_axis(table, tap.astype(jnp.int32), axis=1)
    turned = jnp.take_along_axis(looked, source, axis=0)
    return turned, block + jnp.where(wraps, 1.0, 0.0)


def grid_group(arrived, start, count, table, lhs, rhs):
    lines = lax.broadcasted_iota(jnp.int32, (8, HALF), 0).astype(F32)
    zero = jnp.zeros((16, HALF), BF16)
    for source in range(count):
        message = arrived[start + source].astype(F32)
        for half in range(2):
            slots = message[half * 8 : half * 8 + 8]
            columns = slice((source * 2 + half) * HALF, (source * 2 + half + 1) * HALF)

            def line(index):
                return jnp.broadcast_to(slots[index : index + 1], (8, HALF))

            turned_u, block_u = spread(table, line(2), line(4), lines)
            turned_v, block_v = spread(table, line(3), line(5), lines)
            real, imag = line(0) * turned_u, line(1) * turned_u
            real = jnp.concatenate([real, real], axis=0).astype(BF16)
            imag = jnp.concatenate([imag, imag], axis=0).astype(BF16)
            weight_v = jnp.concatenate([turned_v, turned_v], axis=0).astype(BF16)
            at_u = jnp.concatenate([block_u, block_u - 1.0], axis=0).astype(BF16)
            at_v = jnp.concatenate([block_v, block_v - 1.0], axis=0).astype(BF16)
            for block in range(SUB // 16):
                here = at_u == 2 * block
                lhs[block * 16 : (block + 1) * 16, columns] = jnp.where(here, real, zero)
                lhs[SUB + block * 16 : SUB + (block + 1) * 16, columns] = jnp.where(here, imag, zero)
                rhs[block * 16 : (block + 1) * 16, columns] = jnp.where(at_v == 2 * block, weight_v, zero)


def main_kernel(
    vis_hbm, own_hbm, cells_hbm, taps_hbm, table_hbm, rows_hbm, cols_hbm, v_hbm, u_hbm, last_hbm, twist_hbm, out_ref,
    vis_ref, own_ref, cells_ref, taps_ref, table_ref, rows_ref, cols_ref, v_ref, u_ref, last_ref, twist_ref,
    acc, lhs, rhs, sent, arrived, grid, cross_out, cross_in, out_two, in_two, out_three, in_three,
    final_table, factor, load_sem, send_sem, recv_sem, cross_sem, far_send, far_recv, own_sem,
):
    me, chan = lax.axis_index("img"), lax.axis_index("chan")
    loads = [
        pltpu.make_async_copy(source, target, load_sem.at[index])
        for index, (source, target) in enumerate(
            [
                (vis_hbm, vis_ref), (own_hbm, own_ref), (cells_hbm, cells_ref), (taps_hbm, taps_ref),
                (table_hbm, table_ref), (rows_hbm, rows_ref), (cols_hbm, cols_ref), (twist_hbm.at[me], twist_ref),
                (last_hbm, last_ref), (v_hbm, v_ref), (u_hbm, u_ref),
            ]
        )
    ]
    for load in loads[:4]:
        load.start()
    barrier = pltpu.get_barrier_semaphore()

    place_y, place_x, place_z = me >> 5, me >> 3 & 3, me & 7
    rows_y = [(place_y + step & 3) * 32 for step in range(TORUS[0])]
    rows_x = [(place_x + step & 3) * 8 for step in range(TORUS[1])]
    rows_z = [place_z + step & 7 for step in range(TORUS[2])]

    for far_y, far_x, far_z in FAR_FIRST:
        peer = rows_y[far_y] + rows_x[far_x] + rows_z[far_z]
        pl.semaphore_signal(barrier, inc=1, device_id=(peer, chan), device_id_type=MESH)
    pl.semaphore_signal(barrier, inc=1, device_id=(me, 1 - chan), device_id_type=MESH)
    for load in loads[:4]:
        load.wait()
    for load in loads[4:]:
        load.start()
    bucket(me, vis_ref, own_ref, cells_ref, taps_ref, lhs, rhs, acc)

    def send_block(block):
        for step in range(BLOCK):
            offset = ORDER[block] * BLOCK + step
            if offset:
                pltpu.make_async_remote_copy(
                    src_ref=sent.at[block * BLOCK + step], dst_ref=arrived.at[block * BLOCK + step],
                    send_sem=send_sem, recv_sem=recv_sem.at[block],
                    device_id=((me + offset) & (IMG - 1), chan), device_id_type=MESH,
                ).start()

    self_block = ORDER.index(0)
    own = pltpu.make_async_copy(sent.at[self_block * BLOCK], arrived.at[self_block * BLOCK], own_sem.at[0])
    make_messages(0, acc, sent)
    pl.semaphore_wait(barrier, IMG)
    own.start()
    send_block(0)
    for block in range(1, 8):
        make_messages(block, acc, sent)
        send_block(block)

    for load in loads[4:]:
        load.wait()
    grid[...] = jnp.zeros_like(grid)
    table = table_ref[...].astype(F32)
    own.wait()

    def wait_block(block):
        def wait_count(count):
            span = pl.ds(0, count)
            pltpu.make_async_remote_copy(
                src_ref=sent.at[span], dst_ref=arrived.at[span], send_sem=send_sem, recv_sem=recv_sem.at[block],
                device_id=(me, 1 - chan), device_id_type=MESH,
            ).wait_recv()

        @pl.when(block == self_block)
        def _():
            wait_count(BLOCK - 1)

        @pl.when(block != self_block)
        def _():
            wait_count(BLOCK)

    columns = slice(0, GROUP * CAP)

    def grid_step(group, count):
        for block in range(GROUP // BLOCK):
            wait_block(group * (GROUP // BLOCK) + block)
        grid_group(arrived, group * GROUP, GROUP, table, lhs, rhs)
        grid[...] += dot_nt(lhs[:, columns], rhs[:, columns])
        return count

    lax.fori_loop(0, IMG // GROUP, grid_step, 0)

    both = jnp.concatenate([grid[:SUB, :], grid[SUB:, :]], axis=1)
    high, low = split_pair(both)
    pieces = jnp.concatenate([high, high, low], axis=1)

    cross_out[...] = dot_nn(pieces, v_ref[1 - chan])
    cross = pltpu.make_async_remote_copy(
        src_ref=cross_out, dst_ref=cross_in, send_sem=cross_sem.at[0], recv_sem=cross_sem.at[1],
        device_id=(me, 1 - chan), device_id_type=MESH,
    )
    cross.start()
    mine = dot_nn(pieces, v_ref[chan])
    cross.wait_recv()
    out_two[...] = (mine + cross_in[...]).reshape(IMG, 2, SUB).astype(BF16)

    def complex_dot(table, columns):
        product = dot_nn(table, jnp.concatenate([columns, columns], axis=0))
        real = product[:SUB, :HALF] - product[SUB:, HALF:]
        imag = product[SUB:, :HALF] + product[:SUB, HALF:]
        return real, imag

    def exchange(source, target, phase):
        keep = pltpu.make_async_copy(source.at[me], target.at[me], own_sem.at[1 + phase])
        keep.start()

        for far_y, far_x, far_z in FAR_FIRST:
            peer = rows_y[far_y] + rows_x[far_x] + rows_z[far_z]
            pltpu.make_async_remote_copy(
                src_ref=source.at[peer], dst_ref=target.at[me], send_sem=far_send.at[phase],
                recv_sem=far_recv.at[phase], device_id=(peer, chan), device_id_type=MESH,
            ).start()
        keep.wait()
        span = pl.ds(0, IMG - 1)
        return pltpu.make_async_remote_copy(
            src_ref=source.at[span], dst_ref=target.at[span], send_sem=far_send.at[phase],
            recv_sem=far_recv.at[phase], device_id=(me, 1 - chan), device_id_type=MESH,
        )

    second = exchange(out_two, in_two, 0)
    cosine, sine = twist_ref[0:1, :], twist_ref[1:2, :]
    base_cos, base_sin = last_ref[0], last_ref[1]
    for part, value in enumerate((base_cos * cosine - base_sin * sine, base_sin * cosine + base_cos * sine)):
        high, low = split_pair(value)
        final_table[part * SUB : (part + 1) * SUB, :SUB] = high
        final_table[part * SUB : (part + 1) * SUB, SUB:] = low
    scale = 1.0 / math.sqrt(SUB * IMG * SUB)
    for block in range(2):
        rows = slice(block * HALF, (block + 1) * HALF)
        column = jnp.transpose(jnp.broadcast_to(rows_ref[:, rows], (HALF, HALF)))
        factor[rows, :] = column * cols_ref[...] * scale
    second.wait_recv()
    real, imag = complex_dot(u_ref[...], in_two[...].reshape(SUB, SUB))
    out_three[...] = jnp.concatenate([real, imag], axis=1).reshape(IMG, 2, SUB).astype(BF16)
    third = exchange(out_three, in_three, 1)
    third.wait_recv()
    real, imag = complex_dot(final_table[...], in_three[...].reshape(SUB, SUB))
    out_ref[0] = real * factor[...]
    out_ref[1] = imag * factor[...]

    span = pl.ds(0, IMG - 1)
    pltpu.make_async_remote_copy(
        src_ref=sent.at[span], dst_ref=arrived.at[span], send_sem=send_sem, recv_sem=recv_sem.at[0],
        device_id=(me, 1 - chan), device_id_type=MESH,
    ).wait_send()
    cross.wait_send()
    second.wait_send()
    third.wait_send()


def body(visibilities, owner, cells, taps, kernel, taper_rows, taper_cols):
    v_tables, u_table, last_tables, twists = host_tables()
    return pl.pallas_call(
        main_kernel,
        out_shape=jax.ShapeDtypeStruct((2, SUB, HALF), F32),
        in_specs=[pl.BlockSpec(memory_space=pltpu.HBM)] * 11,
        out_specs=pl.BlockSpec(memory_space=pltpu.VMEM),
        scratch_shapes=[
            pltpu.VMEM((2, VIS), BF16),
            pltpu.VMEM((1, VIS), jnp.int32),
            pltpu.VMEM((2, VIS), jnp.int32),
            pltpu.VMEM((2, VIS), jnp.int32),
            pltpu.VMEM((TAPS, OS), BF16),
            pltpu.VMEM((1, SUB), F32),
            pltpu.VMEM((1, HALF), F32),
            pltpu.VMEM(v_tables.shape, BF16),
            pltpu.VMEM(u_table.shape, BF16),
            pltpu.VMEM(last_tables.shape, F32),
            pltpu.VMEM(twists.shape[1:], F32),
            pltpu.VMEM((4 * IMG, CAP), F32),
            pltpu.VMEM((4 * IMG, CHUNK), BF16),
            pltpu.VMEM((CAP, CHUNK), BF16),
            pltpu.VMEM((IMG, 16, HALF), BF16),
            pltpu.VMEM((IMG, 16, HALF), BF16),
            pltpu.VMEM((2 * SUB, SUB), F32),
            pltpu.VMEM((SUB, SUB), F32),
            pltpu.VMEM((SUB, SUB), F32),
            pltpu.VMEM((IMG, 2, SUB), BF16),
            pltpu.VMEM((IMG, 2, SUB), BF16),
            pltpu.VMEM((IMG, 2, SUB), BF16),
            pltpu.VMEM((IMG, 2, SUB), BF16),
            pltpu.VMEM((2 * SUB, 2 * SUB), BF16),
            pltpu.VMEM((SUB, HALF), F32),
            pltpu.SemaphoreType.DMA((11,)),
            pltpu.SemaphoreType.DMA(()),
            pltpu.SemaphoreType.DMA((IMG // BLOCK,)),
            pltpu.SemaphoreType.DMA((2,)),
            pltpu.SemaphoreType.DMA((2,)),
            pltpu.SemaphoreType.DMA((2,)),
            pltpu.SemaphoreType.DMA((3,)),
        ],
        compiler_params=pltpu.CompilerParams(
            collective_id=0, has_side_effects=True, vmem_limit_bytes=60 * 1024 * 1024
        ),
        name="gridding",
    )(
        visibilities[0], owner.reshape(1, VIS), cells[0], taps[0], kernel.T,
        taper_rows.reshape(1, SUB), taper_cols.reshape(1, HALF),
        jnp.asarray(v_tables), jnp.asarray(u_table), jnp.asarray(last_tables), jnp.asarray(twists),
    )


def solution(mesh):
    return jax.shard_map(
        body,
        mesh=mesh,
        in_specs=(
            P("chan", None, "img"),
            P("chan", "img", None),
            P("chan", None, "img"),
            P("chan", None, "img"),
            P(),
            P("img"),
            P("chan"),
        ),
        out_specs=P(None, "img", "chan"),
        check_vma=False,
    )
```
